32 devices in a mesh: rep: 2 (over x), inst: 4 (over y, core), tp: 4 (over z).
Axes of the slice: x: 2, y: 2, z: 4, core: 2. Of those that a mesh axis runs over, the one named last changes fastest.
Arguments:
- cache_base: bfloat16 [2, 192, 256, 1024], P(None, ('rep', 'inst'), None, 'tp'), parts along dimension 1, may hold values from -6 to 6
- cache_scale: bfloat16 [2, 192, 8, 1024], P(None, ('rep', 'inst'), None, 'tp'), parts along dimension 1, may hold values from 0.29882812 to 2
- outlier_tiles: bfloat16 [2, 192, 32, 1024], P(None, ('rep', 'inst'), None, 'tp'), parts along dimension 1, may hold values from -8 to 8
- outlier_pos: int32 [2, 192], P(None, 'rep'), parts along dimension 1, may hold values from 0 to 7
- lengths: int32 [192], P('rep'), parts along dimension 0, may hold values from 1 to 256, as said below
- new_slot: int32 [192], P('rep'), parts along dimension 0, may hold values from 0 to 95, as said below
- queries: bfloat16 [2, 192, 8192], P(None, ('rep', 'inst'), 'tp'), parts along dimension 1, may hold values from -68 to 68
- new_kv: bfloat16 [2, 2, 192, 1024], P(None, None, ('rep', 'inst'), 'tp'), parts along dimension 2, may hold values from -6 to 6
- out_weight: bfloat16 [8192, 4096], P('tp'), may hold values from -0.0625 to 0.0625
Outputs:
- attn_out: bfloat16 [2, 192, 4096], P(None, ('rep', 'inst')), parts along dimension 1
The draws below stay inside these ranges and needn't reach their ends.
There are 2 independent parts, one for each index of `rep`. The reference program is written for one: setup_inputs(seed, part) draws one part's arguments, and reference() takes and returns one part's arrays. A program takes and returns all parts, laid end to end along the dimension named above; an argument that names none is the same for every part. Nothing has to cross between parts.
Inputs may be any that keep to these rules, and one draw needn't show every extreme that they name: `lengths`: each instance's requests follow a load level of their own; one request has exactly 256 tokens. A permutation of the 96 slots; slot new_slot[r] lies on instance new_slot[r] // 24, request r starts on instance r // 24. A request either keeps its slot or moves to another instance; from one instance to another move either no requests or exactly 2, and some pair moves 2.
All inputs are finite; a program needn't handle non-finite values.
Results may differ from the reference program's by a relative error of at most 0.012.
The reference program's roundings to bfloat16 on the way count: a program that leaves them out, or rounds other values in their place, can miss the bound.
Values may be sent and summed in bfloat16 or wider, within the bound.
A program may use at most 128 MiB of HBM per device.

```python
import math
import jax
import jax.numpy as jnp
from jax import lax

HQ = 64
KVH = 8
HD = 128
DW = 4096
CAP = 256
SLOTS = 24
TILE = 32
MOVE = 2
STEPS = 2
INSTANCES = 4
PAIRS = 4
REQS = 96
TILES = 8


def slot_order(sub_key):
    return jax.random.permutation(sub_key, SLOTS)


def draw_lengths(key, part):
    key = jax.random.fold_in(key, 5)
    first_key, second_key, third_key = jax.random.split(key, 3)
    load_level = jax.random.randint(first_key, (INSTANCES, 1), 1, 5)
    raw_draw = jax.random.randint(second_key, (INSTANCES, SLOTS), 0, CAP)
    counts = (1 + raw_draw * load_level // 4).reshape(REQS)
    chosen = jax.random.randint(third_key, (), 0, REQS)
    return jnp.where(jnp.arange(REQS) == chosen, CAP, counts).astype(jnp.int32)


def draw_new_slot(key, part):
    key = jax.random.fold_in(key, 7)
    first_key, second_key = jax.random.split(key)
    home_order = jax.random.permutation(first_key, INSTANCES)
    orders = jax.vmap(slot_order)(jax.random.split(second_key, INSTANCES))
    migrants = PAIRS * MOVE
    sources = jnp.arange(INSTANCES)[:, None]
    rank_index = jnp.broadcast_to(jnp.arange(migrants)[None, :], (INSTANCES, migrants))
    targets = home_order[(sources + rank_index // MOVE) % INSTANCES]
    from_index = sources * SLOTS + orders[:, :migrants]
    to_index = targets * SLOTS + orders[targets, rank_index]
    result = jnp.arange(REQS).at[from_index.reshape(-1)].set(to_index.reshape(-1))
    return result.astype(jnp.int32)


def draw_queries(key, part):
    key = jax.random.fold_in(key, 9)
    first_key = jax.random.fold_in(key, 0)
    full_shape = (STEPS, REQS, HQ * HD)
    values = jnp.clip(jax.random.normal(first_key, full_shape), -6.0, 6.0)
    return values.astype(jnp.bfloat16)


def plant(values, rng, smallest, largest):
    longest = values.shape.index(max(values.shape))
    spots = []
    for shift in (0, 1):
        where = [jax.random.randint(jax.random.fold_in(rng, axis), (), 0, length) for axis, length in enumerate(values.shape)]
        where[longest] = (where[longest] + shift) % values.shape[longest]
        spots.append(tuple(where))
    return values.at[spots[0]].set(smallest).at[spots[1]].set(largest)


def block_levels(rng, dims, pieces, least, largest):
    loudness = 1.0
    for axis_at, shards_of in pieces:
        steps = jax.random.uniform(jax.random.fold_in(jax.random.fold_in(rng, 6), axis_at), (shards_of,), jnp.float32, least / len(pieces), largest / len(pieces))
        loudness = loudness * jnp.repeat(jnp.exp(steps), dims[axis_at] // shards_of).reshape((-1,) + (1,) * (len(dims) - 1 - axis_at))
    return loudness


def normal_values(own_key, dims, deviation, limit, cuts=(), held_as=jnp.bfloat16):
    drawn = deviation * jax.random.normal(own_key, dims, jnp.float32)
    if cuts:
        drawn = drawn * block_levels(own_key, dims, cuts, -0.22, 0.18)
    return jnp.clip(drawn, -limit, limit).astype(held_as)


def setup_inputs(seed: int = 0, part: int = 0) -> dict:
    arg_keys = jax.random.split(jax.random.key(seed), 10)
    own_keys = jax.random.split(jax.random.fold_in(arg_keys[9], part), 10)
    return {
        "cache_base": normal_values(own_keys[0], (2, REQS, CAP, KVH * HD), 1.0, 6.0, ((1, 4), (3, 4))),
        "cache_scale": jnp.clip(jnp.exp(math.log(2.0) - 1.9010339 * jax.random.uniform(own_keys[1], (2, REQS, TILES, KVH * HD), jnp.float32) ** block_levels(own_keys[1], (2, REQS, TILES, KVH * HD), ((1, 4), (3, 4)), -0.2, 0.2)), 0.29882812, 2.0).astype(jnp.bfloat16),
        "outlier_tiles": normal_values(own_keys[2], (2, REQS, TILE, KVH * HD), 2.0, 8.0, ((1, 4), (3, 4))),
        "outlier_pos": plant(jax.random.randint(own_keys[3], (2, REQS), 0, TILES), jax.random.fold_in(own_keys[3], 1), 0, TILES - 1).astype(jnp.int32),
        "lengths": draw_lengths(jax.random.fold_in(jax.random.fold_in(arg_keys[9], part), 71), part),
        "new_slot": draw_new_slot(jax.random.fold_in(jax.random.fold_in(arg_keys[9], part), 71), part),
        "queries": draw_queries(jax.random.fold_in(jax.random.fold_in(arg_keys[9], part), 71), part),
        "new_kv": normal_values(own_keys[7], (STEPS, 2, REQS, KVH * HD), 1.0, 6.0, ((2, 4), (3, 4))),
        "out_weight": normal_values(arg_keys[8], (HQ * HD, DW), (HQ * HD) ** -0.5, 0.0625, ((0, 4),)),
    }


def dequantize(stored, tile_scale, outlier, tile_pos):
    tile_count = tile_scale.shape[0]
    tile_size = outlier.shape[0]
    blocks = stored.astype(jnp.float32).reshape(tile_count, tile_size, -1) * tile_scale.astype(jnp.float32)[:, None, :]
    outlier_hit = (jnp.arange(tile_count, dtype=jnp.int32) == tile_pos)[:, None, None]
    blocks = blocks + jnp.where(outlier_hit, outlier.astype(jnp.float32)[None], 0.0)
    return blocks.reshape(stored.shape).astype(jnp.bfloat16)

def reference(cache_base, cache_scale, outlier_tiles, outlier_pos, lengths, new_slot, queries, new_kv, out_weight):
    slot_total = new_slot.shape[0]
    source = jnp.zeros((slot_total,), jnp.int32).at[new_slot].set(jnp.arange(slot_total, dtype=jnp.int32))
    group_size = HQ // KVH
    score_scale = 1.0 / math.sqrt(HD)

    def one_slot(slot_index):
        request = source[slot_index]
        key_rows = dequantize(cache_base[0, request], cache_scale[0, request], outlier_tiles[0, request], outlier_pos[0, request])
        value_rows = dequantize(cache_base[1, request], cache_scale[1, request], outlier_tiles[1, request], outlier_pos[1, request])
        length = lengths[request]
        query_rows = queries[:, slot_index].astype(jnp.float32).reshape(STEPS, KVH, group_size, HD)
        fresh_rows = new_kv[:, :, slot_index].astype(jnp.float32)
        fresh_keys = fresh_rows[:, 0].reshape(STEPS, KVH, HD)
        fresh_values = fresh_rows[:, 1].reshape(STEPS, KVH, HD)
        key_heads = key_rows.astype(jnp.float32).reshape(CAP, KVH, HD)
        value_heads = value_rows.astype(jnp.float32).reshape(CAP, KVH, HD)
        cache_scores = jnp.einsum('sgrd,tgd->sgrt', query_rows, key_heads) * score_scale
        cache_scores = jnp.where(jnp.arange(CAP, dtype=jnp.int32) < length, cache_scores, -1e+30)
        new_scores = jnp.einsum('sgrd,ugd->sgru', query_rows, fresh_keys) * score_scale
        visible = jnp.arange(STEPS, dtype=jnp.int32)[None, :] <= jnp.arange(STEPS, dtype=jnp.int32)[:, None]
        new_scores = jnp.where(visible[:, None, None, :], new_scores, -1e+30)
        row_max = jnp.maximum(lax.optimization_barrier(jnp.max(cache_scores, axis=-1)), lax.optimization_barrier(jnp.max(new_scores, axis=-1)))
        exp_cache = jnp.exp(cache_scores - row_max[..., None])
        exp_new = jnp.exp(new_scores - row_max[..., None])
        denominator = lax.optimization_barrier(jnp.sum(exp_cache, axis=-1)) + lax.optimization_barrier(jnp.sum(exp_new, axis=-1))
        weight_cache = (exp_cache / denominator[..., None]).astype(jnp.bfloat16)
        weight_new = (exp_new / denominator[..., None]).astype(jnp.bfloat16)
        context = jnp.einsum('sgrt,tgd->sgrd', weight_cache.astype(jnp.float32), value_heads)
        context = context + jnp.einsum('sgru,ugd->sgrd', weight_new.astype(jnp.float32), fresh_values)
        return context.astype(jnp.bfloat16).reshape(STEPS, HQ * HD)
    contexts = lax.map(one_slot, jnp.arange(slot_total, dtype=jnp.int32))
    flat_ctx = jnp.transpose(contexts, (1, 0, 2)).reshape(STEPS * slot_total, HQ * HD)
    projected = jnp.dot(flat_ctx, out_weight, preferred_element_type=jnp.float32)
    return projected.astype(jnp.bfloat16).reshape(STEPS, slot_total, DW)
```

```python
import functools
import math

import jax
import jax.numpy as jnp
from jax import lax
from jax.experimental import pallas as pl
from jax.experimental.pallas import tpu as pltpu
from jax.sharding import PartitionSpec as P

HD = 128
TILE = 32
MOVE = 2
PARTS = 4
MESH = pl.DeviceIdType.MESH
F32 = jnp.float32
BF16 = jnp.bfloat16


def iota(shape, dim):
    return lax.broadcasted_iota(jnp.int32, shape, dim)


def split(values, size, count):
    quotient = jnp.zeros_like(values)
    for i in range(1, count):
        quotient = quotient + jnp.where(values >= i * size, 1, 0)
    return quotient


def onehot(mask):
    return jnp.where(mask, 1.0, 0.0).astype(BF16)


def nt(a, b):
    return lax.dot_general(a, b, (((1,), (1,)), ((), ())), preferred_element_type=F32)


def nn(a, b):
    return jnp.dot(a, b, preferred_element_type=F32)


def body(
    dims,
    ns_ref, pos_ref, len_ref, q_ref, kv_ref, base_hbm, scale_hbm, outl_hbm, w_hbm,
    out_ref,
    cache, scale, outl, wbuf, qsend, qrecv, q3, kn, c3, lhs,
    msend, mrecv, own, bsend, brecv,
    load_sem, w_sem, qs_sem, qr_sem, ms_sem, mr_sem, bs_sem, br_sem, as_sem, ar_sem,
):
    n_inst, n_tp, slots, steps, chunk, per = dims
    me_i = lax.axis_index("inst")
    me_t = lax.axis_index("tp")
    n_req = ns_ref.shape[1]
    q_width = q_ref.shape[1]
    width = kv_ref.shape[1]
    cap = cache.shape[2]
    tiles = cap // TILE
    heads = width // HD
    group = q_width // width
    rows = q_width // HD * steps
    piece = q_width // PARTS
    block = wbuf.shape[2]
    quarter = block // PARTS
    bucket = steps * MOVE * PARTS
    n_bucket = n_inst * bucket
    flat = steps * slots
    chunks = slots // chunk
    first = me_i * slots

    n_dev = n_inst * n_tp
    me = me_i * n_tp + me_t
    barrier = pltpu.get_barrier_semaphore()

    @pl.loop(1, n_dev)
    def _(offset):
        other = lax.rem(me + offset, n_dev)
        pl.semaphore_signal(
            barrier, inc=1,
            device_id={"inst": other // n_tp, "tp": lax.rem(other, n_tp)},
            device_id_type=MESH,
        )

    def load_cache(which, part):
        span = pl.ds(part * chunk, chunk)
        return pltpu.make_async_copy(
            base_hbm.at[which, span], cache.at[which, span], load_sem.at[which * chunks + part]
        )

    load_scale = pltpu.make_async_copy(scale_hbm, scale, load_sem.at[2 * chunks])
    load_outl = pltpu.make_async_copy(outl_hbm, outl, load_sem.at[2 * chunks + 1])

    def load_weight(k):
        col = lax.rem(me_t + 1 + k, n_tp)
        return pltpu.make_async_copy(
            w_hbm.at[:, pl.ds(pl.multiple_of(col * block, block), block)], wbuf.at[k], w_sem.at[k]
        )

    load_scale.start()
    load_outl.start()
    for which in range(2):
        for part in range(chunks):
            load_cache(which, part).start()
    for k in range(n_tp):
        load_weight(k).start()

    ns = ns_ref[...]
    lane = iota((1, n_req), 1)
    home = split(lane, slots, n_inst)
    dest = split(ns, slots, n_inst)
    code = (home * n_inst + dest).astype(F32)
    row_i = iota((n_req, n_req), 0)
    col_i = iota((n_req, n_req), 1)
    code_all = jnp.broadcast_to(code, (n_req, n_req))
    code_col = jnp.sum(jnp.where(row_i == col_i, code_all, 0.0), axis=1, keepdims=True)
    rank = jnp.sum(
        jnp.where(jnp.logical_and(code_col == code_all, row_i < col_i), 1.0, 0.0),
        axis=0, keepdims=True,
    )

    def bucket_fields(shape, dim):
        index = iota(shape, dim)
        return index >> 4, (index >> 3) & 1, (index >> 2) & 1, index & 3

    b_inst, _, b_rank, _ = bucket_fields((n_bucket, n_req), 0)
    same_rank = jnp.logical_and(rank == b_rank.astype(F32), b_inst != me_i)
    arriving = onehot(same_rank & (home == b_inst) & (dest == me_i))
    leaving = onehot(same_rank & (dest == b_inst) & (home == me_i))

    def slot_rows(count):
        index = iota((count * slots, n_req), 0)
        return index - slots * split(index, slots, count)

    slot_steps = onehot(ns - first == slot_rows(steps))
    slot_kv = onehot(ns - first == slot_rows(2 * steps))
    local = onehot(lane - first == slot_rows(steps))

    def step_of(shape, dim):
        return split(iota(shape, dim), slots, steps)

    def fresh_of(shape, dim):
        index = split(iota(shape, dim), slots, 2 * steps)
        return index >> 1, index & 1

    def keep(mask, values):
        return jnp.where(mask, values, 0.0).astype(BF16)

    shape = (n_bucket, flat)
    _, b_step, _, b_part = bucket_fields(shape, 0)
    pick = keep(b_step == step_of(shape, 1), nt(arriving, slot_steps))
    total = jnp.zeros((n_bucket, piece), F32)
    for x in range(PARTS):
        sel = jnp.where(b_part == x, pick.astype(F32), 0.0).astype(BF16)
        total = total + nn(sel, q_ref[:, x * piece:(x + 1) * piece])
    qsend[:, :, :piece] = total.astype(BF16).reshape(n_inst, bucket, piece)
    shape = (n_bucket, 2 * flat)
    _, b_step, _, b_part = bucket_fields(shape, 0)
    f_step, f_kv = fresh_of(shape, 1)
    pick = jnp.where(b_step == f_step, nt(arriving, slot_kv), 0.0)
    total = jnp.zeros((n_bucket, HD), F32)
    for which in range(2):
        for g in range(heads):
            sel = keep((f_kv == which) & (b_part == which * heads + g), pick)
            total = total + nn(sel, kv_ref[:, g * HD:(g + 1) * HD])
    qsend[:, :, piece:] = total.astype(BF16).reshape(n_inst, bucket, HD)
    qrecv[me_i] = jnp.zeros((bucket, piece + HD), BF16)
    brecv[me_i] = jnp.zeros((n_tp, bucket, quarter), BF16)

    pl.semaphore_wait(barrier, n_dev - 1)

    def query_copy(other, slot):
        return pltpu.make_async_remote_copy(
            src_ref=qsend.at[other], dst_ref=qrecv.at[slot],
            send_sem=qs_sem.at[other], recv_sem=qr_sem.at[slot],
            device_id={"inst": other, "tp": me_t}, device_id_type=MESH,
        )

    for offset in range(1, n_inst):
        query_copy(lax.rem(me_i + offset, n_inst), me_i).start()

    load_scale.wait()
    load_outl.wait()

    def dequantize(which, start):
        scales = scale[which, pl.ds(pl.multiple_of(start * tiles, per * tiles), per * tiles), :]
        scales = scales.astype(F32)
        for i in range(per):
            request = start + i
            place = pos_ref[which, first + request]
            extra = outl[which, request].astype(F32)
            for t in range(tiles):
                values = cache[which, request, t * TILE:(t + 1) * TILE, :].astype(F32)
                values = values * scales[i * tiles + t:i * tiles + t + 1, :]
                values = values + jnp.where(place == t, extra, 0.0)
                cache[which, request, t * TILE:(t + 1) * TILE, :] = values.astype(BF16)

    @pl.loop(0, chunks)
    def _(part):
        load_cache(0, part).wait()

        @pl.loop(0, chunk // per)
        def _(p):
            dequantize(0, part * chunk + p * per)

    for offset in range(1, n_inst):
        other = lax.rem(me_i + offset, n_inst)
        copy = query_copy(other, other)
        copy.wait_send()
        copy.wait_recv()
    got = qrecv[...].reshape(n_bucket, piece + HD)
    shape = (flat, n_bucket)
    _, b_step, _, b_part = bucket_fields(shape, 1)
    moved = jnp.where(b_step == step_of(shape, 0), nt(local, leaving), 0.0)
    shape = (flat, flat)
    stay = keep(step_of(shape, 0) == step_of(shape, 1), nt(local, slot_steps))
    for x in range(PARTS):
        piece_q = nn(stay, q_ref[:, x * piece:(x + 1) * piece])
        piece_q = piece_q + nn(keep(b_part == x, moved), got[:, :piece])
        for hh in range(piece // HD):
            h = x * (piece // HD) + hh
            for s in range(steps):
                row = (h // group) * steps * group + s * group + h % group
                q3[:, row, :] = piece_q[s * slots:(s + 1) * slots, hh * HD:(hh + 1) * HD]
    shape = (flat, 2 * flat)
    f_step, f_kv = fresh_of(shape, 1)
    stay = jnp.where(step_of(shape, 0) == f_step, nt(local, slot_kv), 0.0)
    for which in range(2):
        for g in range(heads):
            fresh = nn(keep(f_kv == which, stay), kv_ref[:, g * HD:(g + 1) * HD])
            fresh = fresh + nn(keep(b_part == which * heads + g, moved), got[:, piece:])
            kn[which, :, g * HD:(g + 1) * HD] = fresh.astype(BF16)

    inverse = 1.0 / math.sqrt(HD)
    head_rows = steps * group
    q_row = iota((per * rows, HD), 0) & (rows - 1)
    n_row = iota((rows, flat), 0) & (head_rows - 1)
    n_step = split(n_row, group, steps)
    n_col = iota((rows, flat), 1)
    n_new = split(n_col, slots, steps)
    n_request = n_col - slots * n_new
    seen = n_new <= n_step
    place_t = iota((rows, cap), 1)

    @pl.loop(0, chunks)
    def _(part):
        load_cache(1, part).wait()

        @pl.loop(0, chunk // per)
        def _(p):
            start = part * chunk + p * per
            dequantize(1, start)
            q = q3[pl.ds(start, per)].reshape(per * rows, HD)
            q = jnp.concatenate(
                [
                    jnp.where((q_row >= g * head_rows) & (q_row < (g + 1) * head_rows), q, 0.0)
                    for g in range(heads)
                ],
                axis=1,
            ).astype(BF16)
            fresh = nt(q, kn[0]) * inverse
            for i in range(per):
                request = start + i
                q_i = q[i * rows:(i + 1) * rows]
                scores = nt(q_i, cache[0, request]) * inverse
                scores = jnp.where(place_t < len_ref[first + request], scores, -1e30)
                new = fresh[i * rows:(i + 1) * rows]
                new = jnp.where(seen & (n_request == request), new, -1e30)
                top = jnp.maximum(
                    jnp.max(scores, axis=1, keepdims=True), jnp.max(new, axis=1, keepdims=True)
                )
                exp_cache = jnp.exp(scores - top)
                exp_new = jnp.exp(new - top)
                scale_by = 1.0 / (
                    jnp.sum(exp_cache, axis=1, keepdims=True)
                    + jnp.sum(exp_new, axis=1, keepdims=True)
                )
                context = nn((exp_cache * scale_by).astype(BF16), cache[1, request])
                context = context + nn((exp_new * scale_by).astype(BF16), kn[1])
                for g in range(heads):
                    c3[request, g * head_rows:(g + 1) * head_rows, :] = context[
                        g * head_rows:(g + 1) * head_rows, g * HD:(g + 1) * HD
                    ]

    shape = (flat, flat)
    stay = keep(step_of(shape, 0) == step_of(shape, 1), nt(slot_steps, local))
    shape = (n_bucket, flat)
    _, b_step, _, _ = bucket_fields(shape, 0)
    move = keep(b_step == step_of(shape, 1), nt(leaving, local))
    for h in range(q_width // HD):
        at = (h // group) * steps * group + h % group
        context = jnp.concatenate([c3[:, at + s * group, :] for s in range(steps)], axis=0)
        context = context.astype(BF16)
        lhs[:flat, h * HD:(h + 1) * HD] = nn(stay, context).astype(BF16)
        lhs[flat:, h * HD:(h + 1) * HD] = nn(move, context).astype(BF16)

    def main_copy(k_slot, other, slot):
        return pltpu.make_async_remote_copy(
            src_ref=msend.at[k_slot], dst_ref=mrecv.at[slot],
            send_sem=ms_sem.at[k_slot], recv_sem=mr_sem.at[slot],
            device_id={"inst": me_i, "tp": other}, device_id_type=MESH,
        )

    def bucket_copy(k_slot, inst, tp, from_inst, from_tp):
        return pltpu.make_async_remote_copy(
            src_ref=bsend.at[k_slot, inst], dst_ref=brecv.at[from_inst, from_tp],
            send_sem=bs_sem.at[k_slot, inst], recv_sem=br_sem.at[from_inst, from_tp],
            device_id={"inst": inst, "tp": tp}, device_id_type=MESH,
        )

    _, _, _, b_part = bucket_fields((n_bucket, quarter), 0)

    def project(k, keep_main):
        load_weight(k).wait()
        moved_rows = jnp.zeros((n_bucket, quarter), F32)
        for x in range(PARTS):
            cols = slice(x * quarter, (x + 1) * quarter)
            part = nn(lhs[...], wbuf[k, :, cols])
            keep_main(x, cols, part[:flat])
            moved_rows = jnp.where(b_part == x, part[flat:], moved_rows)
        bsend[k] = moved_rows.astype(BF16).reshape(n_inst, bucket, quarter)

    def send_buckets(k, tp):
        @pl.loop(1, n_inst)
        def _(offset):
            bucket_copy(k, lax.rem(me_i + offset, n_inst), tp, me_i, me_t).start()

    @pl.loop(0, n_tp - 1)
    def _(k):
        tp = lax.rem(me_t + 1 + k, n_tp)

        def keep_main(x, cols, values):
            msend[k, :, cols] = values.astype(BF16)

        project(k, keep_main)
        main_copy(k, tp, me_t).start()
        send_buckets(k, tp)

    def keep_own(x, cols, values):
        own[:, cols] = values

    project(n_tp - 1, keep_own)
    send_buckets(n_tp - 1, me_t)

    others = [lax.rem(me_t + 1 + k, n_tp) for k in range(n_tp - 1)]
    for k in range(n_tp - 1):
        copy = main_copy(k, others[k], others[k])
        copy.wait_send()
        copy.wait_recv()

    @pl.loop(1, n_inst)
    def _(offset):
        inst = lax.rem(me_i + offset, n_inst)

        @pl.loop(0, n_tp)
        def _(k):
            copy = bucket_copy(k, inst, me_t, inst, k)
            copy.wait_send()
            copy.wait_recv()

    came = jnp.zeros((n_inst, bucket, quarter), F32)
    for t in range(n_tp):
        came = came + brecv[:, t].astype(F32)
    came = came.astype(BF16).reshape(n_bucket, quarter)
    shape = (flat, n_bucket)
    _, b_step, _, b_part2 = bucket_fields(shape, 1)
    put = jnp.where(step_of(shape, 0) == b_step, nt(slot_steps, arriving), 0.0)
    for x in range(PARTS):
        cols = slice(x * quarter, (x + 1) * quarter)
        done = own[:, cols] + nn(keep(b_part2 == x, put), came)
        for tp in others:
            done = done + mrecv[tp, :, cols].astype(F32)
        at = pl.multiple_of(me_t * block + x * quarter, quarter)
        out_ref[:, pl.ds(at, quarter)] = done.astype(BF16)

    def final_copy(k, other, owner):
        span = pl.ds(pl.multiple_of(owner * block, block), block)
        return pltpu.make_async_remote_copy(
            src_ref=out_ref.at[:, span], dst_ref=out_ref.at[:, span],
            send_sem=as_sem.at[k], recv_sem=ar_sem.at[owner],
            device_id={"inst": me_i, "tp": other}, device_id_type=MESH,
        )

    for k in range(n_tp - 1):
        final_copy(k, lax.rem(me_t + 1 + k, n_tp), me_t).start()
    for k in range(n_tp - 1):
        other = lax.rem(me_t + 1 + k, n_tp)
        final_copy(k, other, me_t).wait_send()
        final_copy(k, other, other).wait_recv()


def on_device(
    cache_base, cache_scale, outlier_tiles, outlier_pos, lengths, new_slot, queries, new_kv,
    out_weight,
):
    n_inst = lax.axis_size("inst")
    n_tp = lax.axis_size("tp")
    _, slots, cap, width = cache_base.shape
    steps, _, q_width = queries.shape
    n_req = new_slot.shape[0]
    out_width = out_weight.shape[1]
    tiles = cap // TILE
    chunk, per = 8, 4
    flat = steps * slots
    bucket = steps * MOVE * PARTS
    n_bucket = n_inst * bucket
    rows = q_width // HD * steps
    block = out_width // n_tp
    quarter = block // PARTS
    piece = q_width // PARTS
    chunks = slots // chunk
    vmem = pl.BlockSpec(memory_space=pltpu.VMEM)
    smem = pl.BlockSpec(memory_space=pltpu.SMEM)
    hbm = pl.BlockSpec(memory_space=pl.ANY)
    dma = pltpu.SemaphoreType.DMA
    out = pl.pallas_call(
        functools.partial(body, (n_inst, n_tp, slots, steps, chunk, per)),
        out_shape=jax.ShapeDtypeStruct((flat, out_width), BF16),
        in_specs=[vmem, smem, smem, vmem, vmem, hbm, hbm, hbm, hbm],
        out_specs=vmem,
        scratch_shapes=[
            pltpu.VMEM((2, slots, cap, width), BF16),
            pltpu.VMEM((2, slots * tiles, width), BF16),
            pltpu.VMEM((2, slots, TILE, width), BF16),
            pltpu.VMEM((n_tp, q_width, block), BF16),
            pltpu.VMEM((n_inst, bucket, piece + HD), BF16),
            pltpu.VMEM((n_inst, bucket, piece + HD), BF16),
            pltpu.VMEM((slots, rows, HD), F32),
            pltpu.VMEM((2, flat, width), BF16),
            pltpu.VMEM((slots, rows, HD), F32),
            pltpu.VMEM((flat + n_bucket, q_width), BF16),
            pltpu.VMEM((n_tp, flat, block), BF16),
            pltpu.VMEM((n_tp, flat, block), BF16),
            pltpu.VMEM((flat, block), F32),
            pltpu.VMEM((n_tp, n_inst, bucket, quarter), BF16),
            pltpu.VMEM((n_inst, n_tp, bucket, quarter), BF16),
            dma((2 * chunks + 2,)),
            dma((n_tp,)),
            dma((n_inst,)),
            dma((n_inst,)),
            dma((n_tp,)),
            dma((n_tp,)),
            dma((n_tp, n_inst)),
            dma((n_inst, n_tp)),
            dma((n_tp,)),
            dma((n_tp,)),
        ],
        compiler_params=pltpu.CompilerParams(
            collective_id=0, has_side_effects=True, vmem_limit_bytes=48 * 1024 * 1024
        ),
    )(
        new_slot.reshape(1, n_req),
        outlier_pos,
        lengths,
        queries.reshape(flat, q_width),
        new_kv.reshape(2 * flat, width),
        cache_base,
        cache_scale.reshape(2, slots * tiles, width),
        outlier_tiles,
        out_weight,
    )
    return out.reshape(steps, slots, out_width)


def solution(mesh):
    placed = (
        P(None, ("rep", "inst"), None, "tp"),
        P(None, ("rep", "inst"), None, "tp"),
        P(None, ("rep", "inst"), None, "tp"),
        P(None, "rep"),
        P("rep"),
        P("rep"),
        P(None, ("rep", "inst"), "tp"),
        P(None, None, ("rep", "inst"), "tp"),
        P("tp", None),
    )
    return jax.shard_map(
        on_device,
        mesh=mesh,
        in_specs=placed,
        out_specs=P(None, ("rep", "inst"), None),
        check_vma=False,
    )
```

```python
import functools
import math

import jax
import jax.numpy as jnp
from jax import lax
from jax.experimental import pallas as pl
from jax.experimental.pallas import tpu as pltpu
from jax.sharding import PartitionSpec as P

HD = 128
TILE = 32
MOVE = 2
PARTS = 4
MESH = pl.DeviceIdType.MESH
F32 = jnp.float32
BF16 = jnp.bfloat16


def iota(shape, dim):
    return lax.broadcasted_iota(jnp.int32, shape, dim)


def split(values, size, count):
    quotient = jnp.zeros_like(values)
    for i in range(1, count):
        quotient = quotient + jnp.where(values >= i * size, 1, 0)
    return quotient


def onehot(mask):
    return jnp.where(mask, 1.0, 0.0).astype(BF16)


def nt(a, b):
    return lax.dot_general(a, b, (((1,), (1,)), ((), ())), preferred_element_type=F32)


def nn(a, b):
    return jnp.dot(a, b, preferred_element_type=F32)


def body(
    dims,
    ns_hbm, pos_hbm, len_hbm, q_hbm, kv_hbm, base_hbm, scale_hbm, outl_hbm, w_hbm,
    out_ref,
    ns_ref, pos_ref, len_ref, q_ref, kv_ref, cache, scale, outl, wbuf, qsend, qrecv, q3, kn, c3, lhs,
    msend, mrecv, own, bsend, brecv,
    small_sem, load_sem, w_sem, qs_sem, qr_sem, ms_sem, mr_sem, bs_sem, br_sem, as_sem, ar_sem,
):
    n_inst, n_tp, slots, steps, chunk, per = dims
    me_i = lax.axis_index("inst")
    me_t = lax.axis_index("tp")
    n_req = ns_ref.shape[1]
    q_width = q_ref.shape[1]
    width = kv_ref.shape[1]
    cap = cache.shape[2]
    tiles = cap // TILE
    heads = width // HD
    group = q_width // width
    rows = q_width // HD * steps
    piece = q_width // PARTS
    block = wbuf.shape[2]
    quarter = block // PARTS
    bucket = steps * MOVE * PARTS
    n_bucket = n_inst * bucket
    flat = steps * slots
    chunks = slots // chunk
    first = me_i * slots

    small = [
        pltpu.make_async_copy(src, dst, small_sem.at[i])
        for i, (src, dst) in enumerate(
            [(ns_hbm, ns_ref), (q_hbm, q_ref), (kv_hbm, kv_ref), (pos_hbm, pos_ref),
             (len_hbm, len_ref)]
        )
    ]
    for copy in small:
        copy.start()
    n_dev = n_inst * n_tp
    me = me_i * n_tp + me_t
    barrier = pltpu.get_barrier_semaphore()

    @pl.loop(1, n_dev)
    def _(offset):
        other = lax.rem(me + offset, n_dev)
        pl.semaphore_signal(
            barrier, inc=1,
            device_id={"inst": other // n_tp, "tp": lax.rem(other, n_tp)},
            device_id_type=MESH,
        )

    def load_cache(which, part):
        span = pl.ds(part * chunk, chunk)
        return pltpu.make_async_copy(
            base_hbm.at[which, span], cache.at[which, span], load_sem.at[which * chunks + part]
        )

    load_scale = pltpu.make_async_copy(scale_hbm, scale, load_sem.at[2 * chunks])
    load_outl = pltpu.make_async_copy(outl_hbm, outl, load_sem.at[2 * chunks + 1])

    def load_weight(k):
        col = lax.rem(me_t + 1 + k, n_tp)
        return pltpu.make_async_copy(
            w_hbm.at[:, pl.ds(pl.multiple_of(col * block, block), block)], wbuf.at[k], w_sem.at[k]
        )

    load_scale.start()
    load_outl.start()
    for which in range(2):
        for part in range(chunks):
            load_cache(which, part).start()
    for k in range(n_tp):
        load_weight(k).start()

    small[0].wait()
    ns = ns_ref[...]
    lane = iota((1, n_req), 1)
    home = split(lane, slots, n_inst)
    dest = split(ns, slots, n_inst)
    code = (home * n_inst + dest).astype(F32)
    row_i = iota((n_req, n_req), 0)
    col_i = iota((n_req, n_req), 1)
    code_all = jnp.broadcast_to(code, (n_req, n_req))
    code_col = jnp.sum(jnp.where(row_i == col_i, code_all, 0.0), axis=1, keepdims=True)
    rank = jnp.sum(
        jnp.where(jnp.logical_and(code_col == code_all, row_i < col_i), 1.0, 0.0),
        axis=0, keepdims=True,
    )

    def bucket_fields(shape, dim):
        index = iota(shape, dim)
        return index >> 4, (index >> 3) & 1, (index >> 2) & 1, index & 3

    b_inst, _, b_rank, _ = bucket_fields((n_bucket, n_req), 0)
    same_rank = jnp.logical_and(rank == b_rank.astype(F32), b_inst != me_i)
    arriving = onehot(same_rank & (home == b_inst) & (dest == me_i))
    leaving = onehot(same_rank & (dest == b_inst) & (home == me_i))

    def slot_rows(count):
        index = iota((count * slots, n_req), 0)
        return index - slots * split(index, slots, count)

    slot_steps = onehot(ns - first == slot_rows(steps))
    slot_kv = onehot(ns - first == slot_rows(2 * steps))
    local = onehot(lane - first == slot_rows(steps))

    def step_of(shape, dim):
        return split(iota(shape, dim), slots, steps)

    def fresh_of(shape, dim):
        index = split(iota(shape, dim), slots, 2 * steps)
        return index >> 1, index & 1

    def keep(mask, values):
        return jnp.where(mask, values, 0.0).astype(BF16)

    small[1].wait()
    small[2].wait()
    shape = (n_bucket, flat)
    _, b_step, _, b_part = bucket_fields(shape, 0)
    pick = keep(b_step == step_of(shape, 1), nt(arriving, slot_steps))
    total = jnp.zeros((n_bucket, piece), F32)
    for x in range(PARTS):
        sel = jnp.where(b_part == x, pick.astype(F32), 0.0).astype(BF16)
        total = total + nn(sel, q_ref[:, x * piece:(x + 1) * piece])
    qsend[:, :, :piece] = total.astype(BF16).reshape(n_inst, bucket, piece)
    shape = (n_bucket, 2 * flat)
    _, b_step, _, b_part = bucket_fields(shape, 0)
    f_step, f_kv = fresh_of(shape, 1)
    pick = jnp.where(b_step == f_step, nt(arriving, slot_kv), 0.0)
    total = jnp.zeros((n_bucket, HD), F32)
    for which in range(2):
        for g in range(heads):
            sel = keep((f_kv == which) & (b_part == which * heads + g), pick)
            total = total + nn(sel, kv_ref[:, g * HD:(g + 1) * HD])
    qsend[:, :, piece:] = total.astype(BF16).reshape(n_inst, bucket, HD)
    qrecv[me_i] = jnp.zeros((bucket, piece + HD), BF16)
    brecv[me_i] = jnp.zeros((n_tp, bucket, quarter), BF16)

    pl.semaphore_wait(barrier, n_dev - 1)

    def query_copy(other, slot):
        return pltpu.make_async_remote_copy(
            src_ref=qsend.at[other], dst_ref=qrecv.at[slot],
            send_sem=qs_sem.at[other], recv_sem=qr_sem.at[slot],
            device_id={"inst": other, "tp": me_t}, device_id_type=MESH,
        )

    for offset in range(1, n_inst):
        query_copy(lax.rem(me_i + offset, n_inst), me_i).start()

    small[3].wait()
    small[4].wait()
    load_scale.wait()
    load_outl.wait()

    def dequantize(which, start):
        scales = scale[which, pl.ds(pl.multiple_of(start * tiles, per * tiles), per * tiles), :]
        scales = scales.astype(F32)
        for i in range(per):
            request = start + i
            place = pos_ref[which, first + request]
            extra = outl[which, request].astype(F32)
            for t in range(tiles):
                values = cache[which, request, t * TILE:(t + 1) * TILE, :].astype(F32)
                values = values * scales[i * tiles + t:i * tiles + t + 1, :]
                values = values + jnp.where(place == t, extra, 0.0)
                cache[which, request, t * TILE:(t + 1) * TILE, :] = values.astype(BF16)

    @pl.loop(0, chunks)
    def _(part):
        load_cache(0, part).wait()

        @pl.loop(0, chunk // per)
        def _(p):
            dequantize(0, part * chunk + p * per)

    for offset in range(1, n_inst):
        other = lax.rem(me_i + offset, n_inst)
        copy = query_copy(other, other)
        copy.wait_send()
        copy.wait_recv()
    got = qrecv[...].reshape(n_bucket, piece + HD)
    shape = (flat, n_bucket)
    _, b_step, _, b_part = bucket_fields(shape, 1)
    moved = jnp.where(b_step == step_of(shape, 0), nt(local, leaving), 0.0)
    shape = (flat, flat)
    stay = keep(step_of(shape, 0) == step_of(shape, 1), nt(local, slot_steps))
    for x in range(PARTS):
        piece_q = nn(stay, q_ref[:, x * piece:(x + 1) * piece])
        piece_q = piece_q + nn(keep(b_part == x, moved), got[:, :piece])
        for hh in range(piece // HD):
            h = x * (piece // HD) + hh
            for s in range(steps):
                row = (h // group) * steps * group + s * group + h % group
                q3[:, row, :] = piece_q[s * slots:(s + 1) * slots, hh * HD:(hh + 1) * HD]
    shape = (flat, 2 * flat)
    f_step, f_kv = fresh_of(shape, 1)
    stay = jnp.where(step_of(shape, 0) == f_step, nt(local, slot_kv), 0.0)
    for which in range(2):
        for g in range(heads):
            fresh = nn(keep(f_kv == which, stay), kv_ref[:, g * HD:(g + 1) * HD])
            fresh = fresh + nn(keep(b_part == which * heads + g, moved), got[:, piece:])
            kn[which, :, g * HD:(g + 1) * HD] = fresh.astype(BF16)

    inverse = 1.0 / math.sqrt(HD)
    head_rows = steps * group
    q_row = iota((per * rows, HD), 0) & (rows - 1)
    n_row = iota((rows, flat), 0) & (head_rows - 1)
    n_step = split(n_row, group, steps)
    n_col = iota((rows, flat), 1)
    n_new = split(n_col, slots, steps)
    n_request = n_col - slots * n_new
    seen = n_new <= n_step
    place_t = iota((rows, cap), 1)

    @pl.loop(0, chunks)
    def _(part):
        load_cache(1, part).wait()

        @pl.loop(0, chunk // per)
        def _(p):
            start = part * chunk + p * per
            dequantize(1, start)
            q = q3[pl.ds(start, per)].reshape(per * rows, HD)
            q = jnp.concatenate(
                [
                    jnp.where((q_row >= g * head_rows) & (q_row < (g + 1) * head_rows), q, 0.0)
                    for g in range(heads)
                ],
                axis=1,
            ).astype(BF16)
            fresh = nt(q, kn[0]) * inverse
            for i in range(per):
                request = start + i
                q_i = q[i * rows:(i + 1) * rows]
                scores = nt(q_i, cache[0, request]) * inverse
                scores = jnp.where(place_t < len_ref[first + request], scores, -1e30)
                new = fresh[i * rows:(i + 1) * rows]
                new = jnp.where(seen & (n_request == request), new, -1e30)
                top = jnp.maximum(
                    jnp.max(scores, axis=1, keepdims=True), jnp.max(new, axis=1, keepdims=True)
                )
                exp_cache = jnp.exp(scores - top)
                exp_new = jnp.exp(new - top)
                scale_by = 1.0 / (
                    jnp.sum(exp_cache, axis=1, keepdims=True)
                    + jnp.sum(exp_new, axis=1, keepdims=True)
                )
                context = nn((exp_cache * scale_by).astype(BF16), cache[1, request])
                context = context + nn((exp_new * scale_by).astype(BF16), kn[1])
                for g in range(heads):
                    c3[request, g * head_rows:(g + 1) * head_rows, :] = context[
                        g * head_rows:(g + 1) * head_rows, g * HD:(g + 1) * HD
                    ]

    shape = (flat, flat)
    stay = keep(step_of(shape, 0) == step_of(shape, 1), nt(slot_steps, local))
    shape = (n_bucket, flat)
    _, b_step, _, _ = bucket_fields(shape, 0)
    move = keep(b_step == step_of(shape, 1), nt(leaving, local))
    for h in range(q_width // HD):
        at = (h // group) * steps * group + h % group
        context = jnp.concatenate([c3[:, at + s * group, :] for s in range(steps)], axis=0)
        context = context.astype(BF16)
        lhs[:flat, h * HD:(h + 1) * HD] = nn(stay, context).astype(BF16)
        lhs[flat:, h * HD:(h + 1) * HD] = nn(move, context).astype(BF16)

    def main_copy(k_slot, other, slot):
        return pltpu.make_async_remote_copy(
            src_ref=msend.at[k_slot], dst_ref=mrecv.at[slot],
            send_sem=ms_sem.at[k_slot], recv_sem=mr_sem.at[slot],
            device_id={"inst": me_i, "tp": other}, device_id_type=MESH,
        )

    def bucket_copy(k_slot, inst, tp, from_inst, from_tp):
        return pltpu.make_async_remote_copy(
            src_ref=bsend.at[k_slot, inst], dst_ref=brecv.at[from_inst, from_tp],
            send_sem=bs_sem.at[k_slot, inst], recv_sem=br_sem.at[from_inst, from_tp],
            device_id={"inst": inst, "tp": tp}, device_id_type=MESH,
        )

    _, _, _, b_part = bucket_fields((n_bucket, quarter), 0)

    def project(k, keep_main):
        load_weight(k).wait()
        moved_rows = jnp.zeros((n_bucket, quarter), F32)
        for x in range(PARTS):
            cols = slice(x * quarter, (x + 1) * quarter)
            part = nn(lhs[...], wbuf[k, :, cols])
            keep_main(x, cols, part[:flat])
            moved_rows = jnp.where(b_part == x, part[flat:], moved_rows)
        bsend[k] = moved_rows.astype(BF16).reshape(n_inst, bucket, quarter)

    def send_buckets(k, tp):
        @pl.loop(1, n_inst)
        def _(offset):
            bucket_copy(k, lax.rem(me_i + offset, n_inst), tp, me_i, me_t).start()

    @pl.loop(0, n_tp - 1)
    def _(k):
        tp = lax.rem(me_t + 1 + k, n_tp)

        def keep_main(x, cols, values):
            msend[k, :, cols] = values.astype(BF16)

        project(k, keep_main)
        main_copy(k, tp, me_t).start()
        send_buckets(k, tp)

    def keep_own(x, cols, values):
        own[:, cols] = values

    project(n_tp - 1, keep_own)
    send_buckets(n_tp - 1, me_t)

    others = [lax.rem(me_t + 1 + k, n_tp) for k in range(n_tp - 1)]
    for k in range(n_tp - 1):
        copy = main_copy(k, others[k], others[k])
        copy.wait_send()
        copy.wait_recv()

    @pl.loop(1, n_inst)
    def _(offset):
        inst = lax.rem(me_i + offset, n_inst)

        @pl.loop(0, n_tp)
        def _(k):
            copy = bucket_copy(k, inst, me_t, inst, k)
            copy.wait_send()
            copy.wait_recv()

    came = jnp.zeros((n_inst, bucket, quarter), F32)
    for t in range(n_tp):
        came = came + brecv[:, t].astype(F32)
    came = came.astype(BF16).reshape(n_bucket, quarter)
    shape = (flat, n_bucket)
    _, b_step, _, b_part2 = bucket_fields(shape, 1)
    put = jnp.where(step_of(shape, 0) == b_step, nt(slot_steps, arriving), 0.0)
    for x in range(PARTS):
        cols = slice(x * quarter, (x + 1) * quarter)
        done = own[:, cols] + nn(keep(b_part2 == x, put), came)
        for tp in others:
            done = done + mrecv[tp, :, cols].astype(F32)
        at = pl.multiple_of(me_t * block + x * quarter, quarter)
        out_ref[:, pl.ds(at, quarter)] = done.astype(BF16)

    def final_copy(k, other, owner):
        span = pl.ds(pl.multiple_of(owner * block, block), block)
        return pltpu.make_async_remote_copy(
            src_ref=out_ref.at[:, span], dst_ref=out_ref.at[:, span],
            send_sem=as_sem.at[k], recv_sem=ar_sem.at[owner],
            device_id={"inst": me_i, "tp": other}, device_id_type=MESH,
        )

    for k in range(n_tp - 1):
        final_copy(k, lax.rem(me_t + 1 + k, n_tp), me_t).start()
    for k in range(n_tp - 1):
        other = lax.rem(me_t + 1 + k, n_tp)
        final_copy(k, other, me_t).wait_send()
        final_copy(k, other, other).wait_recv()


def on_device(
    cache_base, cache_scale, outlier_tiles, outlier_pos, lengths, new_slot, queries, new_kv,
    out_weight,
):
    n_inst = lax.axis_size("inst")
    n_tp = lax.axis_size("tp")
    _, slots, cap, width = cache_base.shape
    steps, _, q_width = queries.shape
    n_req = new_slot.shape[0]
    out_width = out_weight.shape[1]
    tiles = cap // TILE
    chunk, per = 8, 4
    flat = steps * slots
    bucket = steps * MOVE * PARTS
    n_bucket = n_inst * bucket
    rows = q_width // HD * steps
    block = out_width // n_tp
    quarter = block // PARTS
    piece = q_width // PARTS
    chunks = slots // chunk
    vmem = pl.BlockSpec(memory_space=pltpu.VMEM)
    hbm = pl.BlockSpec(memory_space=pl.ANY)
    dma = pltpu.SemaphoreType.DMA
    out = pl.pallas_call(
        functools.partial(body, (n_inst, n_tp, slots, steps, chunk, per)),
        out_shape=jax.ShapeDtypeStruct((flat, out_width), BF16),
        in_specs=[hbm] * 9,
        out_specs=vmem,
        scratch_shapes=[
            pltpu.VMEM((1, n_req), jnp.int32),
            pltpu.SMEM((2, n_req), jnp.int32),
            pltpu.SMEM((n_req,), jnp.int32),
            pltpu.VMEM((flat, q_width), BF16),
            pltpu.VMEM((2 * flat, width), BF16),
            pltpu.VMEM((2, slots, cap, width), BF16),
            pltpu.VMEM((2, slots * tiles, width), BF16),
            pltpu.VMEM((2, slots, TILE, width), BF16),
            pltpu.VMEM((n_tp, q_width, block), BF16),
            pltpu.VMEM((n_inst, bucket, piece + HD), BF16),
            pltpu.VMEM((n_inst, bucket, piece + HD), BF16),
            pltpu.VMEM((slots, rows, HD), F32),
            pltpu.VMEM((2, flat, width), BF16),
            pltpu.VMEM((slots, rows, HD), F32),
            pltpu.VMEM((flat + n_bucket, q_width), BF16),
            pltpu.VMEM((n_tp, flat, block), BF16),
            pltpu.VMEM((n_tp, flat, block), BF16),
            pltpu.VMEM((flat, block), F32),
            pltpu.VMEM((n_tp, n_inst, bucket, quarter), BF16),
            pltpu.VMEM((n_inst, n_tp, bucket, quarter), BF16),
            dma((5,)),
            dma((2 * chunks + 2,)),
            dma((n_tp,)),
            dma((n_inst,)),
            dma((n_inst,)),
            dma((n_tp,)),
            dma((n_tp,)),
            dma((n_tp, n_inst)),
            dma((n_inst, n_tp)),
            dma((n_tp,)),
            dma((n_tp,)),
        ],
        compiler_params=pltpu.CompilerParams(
            collective_id=0, has_side_effects=True, vmem_limit_bytes=63 * 1024 * 1024
        ),
    )(
        new_slot.reshape(1, n_req),
        outlier_pos,
        lengths,
        queries.reshape(flat, q_width),
        new_kv.reshape(2 * flat, width),
        cache_base,
        cache_scale.reshape(2, slots * tiles, width),
        outlier_tiles,
        out_weight,
    )
    return out.reshape(steps, slots, out_width)


def solution(mesh):
    placed = (
        P(None, ("rep", "inst"), None, "tp"),
        P(None, ("rep", "inst"), None, "tp"),
        P(None, ("rep", "inst"), None, "tp"),
        P(None, "rep"),
        P("rep"),
        P("rep"),
        P(None, ("rep", "inst"), "tp"),
        P(None, None, ("rep", "inst"), "tp"),
        P("tp", None),
    )
    return jax.shard_map(
        on_device,
        mesh=mesh,
        in_specs=placed,
        out_specs=P(None, ("rep", "inst"), None),
        check_vma=False,
    )
```
